128 devices in a mesh: ep: 32 (over y, z, core), tp: 4 (over x).
Axes of the slice: x: 4, y: 4, z: 4, core: 2. Of those that a mesh axis runs over, the one named last changes fastest.
Arguments:
- residual: bfloat16 [4096, 4096], P('ep'), may hold values from -5 to 5
- queries: bfloat16 [4096, 4096], P('ep', 'tp'), may hold values from -120 to 120
- new_keys: bfloat16 [4096, 512], P('ep', 'tp'), may hold values from -4 to 4
- new_values: bfloat16 [4096, 512], P('ep', 'tp'), may hold values from -4 to 4
- cache_keys: bfloat16 [128, 1024, 512], P('ep', None, 'tp'), may hold values from -4 to 4
- cache_values: bfloat16 [128, 1024, 512], P('ep', None, 'tp'), may hold values from -4 to 4
- new_count: int32 [128], P('ep'), may hold values from 2 to 64, as said below
- cached_len: int32 [128], P('ep'), may hold values from 128 to 1024, as said below
- out_proj: bfloat16 [4096, 4096], P('tp'), may hold values from -0.75 to 0.75
- norm_gain: bfloat16 [4096], replicated, may hold values from 0.099609375 to 1.8984375
- expert_ids: int32 [4096, 8], P('ep'), may hold values from 0 to 63, all different within a row; in each aligned block of 128 rows (0 to 127, 128 to 255, ...) at most 32 rows name the same one
- gate_scale: float32 [4096, 8], P('ep'), may hold values from 0.02 to 0.3
- w_gate: bfloat16 [64, 4096, 768], P('ep', None, 'tp'), may hold values from -0.09375 to 0.09375
- w_up: bfloat16 [64, 4096, 768], P('ep', None, 'tp'), may hold values from -0.09375 to 0.09375
- w_down: bfloat16 [64, 768, 4096], P('ep', 'tp'), may hold values from -0.21875 to 0.21875
Outputs:
- layer_out: bfloat16 [4096, 4096], P('ep', 'tp')
The draws below stay inside these ranges and needn't reach their ends.
Inputs may be any that keep to these rules, and one draw needn't show every extreme that they name: `new_count`: each count is even; the counts of a group's 4 conversations sum to 128, and one of them is 64. `cached_len`: in every group one conversation has 1024. `expert_ids`: 8 different experts a token; among the 128 tokens of one group no expert is named more than 32 times.
All inputs are finite; a program needn't handle non-finite values.
Results may differ from the reference program's by a relative error of at most 0.02.
Values may be sent and summed in bfloat16 or wider, within the bound.
No kernel may reach another device: no remote copies, remote signals or barrier semaphores. Data moves between devices by JAX's collectives and lax.ppermute only.
A program may use at most 128 MiB of HBM per device.

```python
import math
import jax
import jax.numpy as jnp
import numpy as np
from jax import lax

D = 4096
HEADS = 32
KVH = 4
HD = 128
FFW = 768
TOPK = 8
TOK_GRP = 128
CONV_GRP = 4
CACHE = 1024
TOKENS = 4096
CONVS = 128
EXPERTS = 64
CAP = 32
N_TP = 4


def shared_keys(key):
    base = jnp.clip(jax.random.normal(jax.random.fold_in(key, 101), (TOKENS, KVH * HD), jnp.float32), -4.0, 4.0)
    return base


def draw_new_keys(key, part):
    base = shared_keys(key)
    return base.astype(jnp.bfloat16)


def draw_queries(key, part):
    key = jax.random.fold_in(key, 4)
    drawn = jnp.clip(jax.random.normal(key, (TOKENS, HEADS * HD), jnp.float32), -4.0, 4.0)
    return drawn.astype(jnp.bfloat16)


def draw_residual(key, part):
    key = jax.random.fold_in(key, 5)
    key_one, key_two, key_three = jax.random.split(key, 3)
    columns = jnp.arange(D, dtype=jnp.float32) / D
    rough = jax.random.uniform(key_two, (D,), jnp.float32, 0.7, 1.4)
    noise = jnp.clip(jax.random.normal(key_one, (TOKENS, D), jnp.float32), -2.5, 2.5)
    column_scale = 0.05 * jnp.power(10.0, columns) * rough
    row_scale = jnp.exp(jax.random.uniform(key_three, (TOKENS, 1), jnp.float32, math.log(0.5), math.log(2.0)))
    return (noise * column_scale[None, :] * row_scale).astype(jnp.bfloat16)


def draw_new_count(key, part):
    key = jax.random.fold_in(key, 11)
    groups = CONVS // CONV_GRP
    keys_all = jax.random.split(key, groups)
    halves = TOK_GRP // 4

    def one_group(group_key):
        key_cut, key_order = jax.random.split(group_key)
        cuts = jax.random.permutation(key_cut, halves - 1)[:2] + 1
        lower = jnp.min(cuts)
        upper = jnp.max(cuts)
        counts = jnp.stack([jnp.array(TOK_GRP // 2, jnp.int32), (2 * lower).astype(jnp.int32), (2 * (upper - lower)).astype(jnp.int32), (2 * (halves - upper)).astype(jnp.int32)])
        order = jax.random.permutation(key_order, 4)
        return counts[order]
    return jax.vmap(one_group)(keys_all).reshape(-1).astype(jnp.int32)


def draw_cached_len(key, part):
    key = jax.random.fold_in(key, 12)
    groups = CONVS // CONV_GRP
    key_len, key_pick = jax.random.split(key)
    lengths = jax.random.randint(key_len, (groups, CONV_GRP), CACHE // 8, CACHE + 1)
    chosen = jax.random.randint(key_pick, (groups, 1), 0, CONV_GRP)
    lengths = jnp.where(jnp.arange(CONV_GRP)[None, :] == chosen, CACHE, lengths)
    return lengths.reshape(-1).astype(jnp.int32)


def steps_of(key, shape, cuts, smallest, largest):
    factor_of = 1.0
    for dim, parts in cuts:
        steps = jax.random.uniform(jax.random.fold_in(jax.random.fold_in(key, 6), dim), (parts,), jnp.float32, smallest / len(cuts), largest / len(cuts))
        factor_of = factor_of * jnp.repeat(jnp.exp(steps), shape[dim] // parts).reshape((-1,) + (1,) * (len(shape) - 1 - dim))
    return factor_of


def routed_block(rng, own, number, rows, number_of, top, bound, slope):
    order = jax.random.permutation(rng, number_of)
    packed, ordinary = load_shares(number_of, rows * top, bound, slope, True), load_shares(number_of, rows * top, bound, slope, False)
    places = jnp.arange(number_of)

    def named(tallies, turn):
        used = int((tallies > 0).sum())
        fixed = max(1, used // 4)
        passed = fixed + (places - fixed + turn * (used - fixed)) % max(1, number_of - fixed)
        return jnp.zeros((number_of,), jnp.int32).at[order[jnp.where(places < fixed, places, passed)]].set(jnp.asarray(tallies, jnp.int32))

    tallies = jnp.where(number % 4 == 0, named(packed, number // 4), named(ordinary, number - number // 4 - 1))
    mixed = jax.random.permutation(jax.random.fold_in(own, 3), number_of)
    giver, receiver = mixed[0:number_of // 2 * 2:2], mixed[1:number_of // 2 * 2:2]
    room = jnp.minimum(tallies[giver] - 1, bound - tallies[receiver]) // 2
    room = jnp.where((giver == order[0]) | (receiver == order[0]) | (tallies[receiver] == 0), 0, jnp.maximum(room, 0))
    passed = jax.random.randint(jax.random.fold_in(own, 4), (number_of // 2,), 0, 1 << 20) % (room + 1)
    tallies = tallies.at[giver].add(-passed).at[receiver].add(passed)
    members = jnp.searchsorted(jnp.cumsum(tallies), jnp.arange(rows * top), side="right").astype(jnp.int32)
    table = members.reshape(top, rows).T
    table = table[jax.random.permutation(jax.random.fold_in(own, 1), rows)]
    turn = jax.random.randint(jax.random.fold_in(own, 2), (rows, 1), 0, top)
    return jnp.take_along_axis(table, (jnp.arange(top)[None, :] + turn) % top, axis=1)


def load_shares(amount, total, reach, slope, full):
    portions = [(1 << 20) // math.isqrt(rank ** slope) + 1 for rank in range(1, amount + 1)]
    largest = reach if full else min(reach, max(-(-total // amount), total * portions[0] // sum(portions)))
    least = 1 if total - largest >= amount - 1 else 0
    given, rest = [largest] + [least] * (amount - 1), total - largest - least * (amount - 1)
    while rest > 0:
        free = [i for i in range(1, amount) if given[i] < largest] or [i for i in range(1, amount) if given[i] < reach]
        whole, budget = sum([portions[i] for i in free]), rest
        for i in free:
            more = min(reach - given[i], max(1, budget * portions[i] // whole), rest)
            given[i] = given[i] + more
            rest = rest - more
    return np.array(given)


def gaussian(rng, shape, spread, limit, cuts=(), kind=jnp.bfloat16):
    gain = steps_of(rng, shape, cuts, -0.22, 0.18) if cuts else 1.0
    values = jax.random.normal(rng, shape, jnp.float32) * spread * gain
    return jnp.minimum(jnp.maximum(values, -limit), limit).astype(kind)


def setup_inputs(seed: int = 0) -> dict:
    splits = jax.random.split(jax.random.key(seed), 16)
    residual = draw_residual(jax.random.fold_in(splits[15], 71), 0)
    queries = draw_queries(jax.random.fold_in(splits[15], 71), 0)
    new_keys = draw_new_keys(jax.random.fold_in(splits[15], 71), 0)
    new_values = gaussian(splits[3], (TOKENS, KVH * HD), 1.0, 4.0, ((0, 32), (1, 4)))
    cache_keys = gaussian(splits[4], (CONVS, CACHE, KVH * HD), 1.0, 4.0, ((0, 32), (2, 4)))
    cache_values = gaussian(splits[5], (CONVS, CACHE, KVH * HD), 1.0, 4.0, ((0, 32), (2, 4)))
    new_count = draw_new_count(jax.random.fold_in(splits[15], 71), 0)
    cached_len = draw_cached_len(jax.random.fold_in(splits[15], 71), 0)
    out_proj = gaussian(splits[8], (HEADS * HD, D), (HD // 2) ** -0.5, 0.75, ((0, 4),))
    norm_gain = jnp.clip(1.0 + 0.18 * jax.random.normal(splits[9], (D,), jnp.float32), 0.099609375, 1.8984375).astype(jnp.bfloat16)
    expert_ids_keys = jax.random.split(jax.random.fold_in(splits[10], 1), TOKENS // TOK_GRP)
    expert_ids_turns = jax.random.permutation(jax.random.fold_in(splits[10], 3), TOKENS // TOK_GRP)
    expert_ids = jax.vmap(lambda own, number: routed_block(jax.random.fold_in(splits[10], 2), own, number, TOK_GRP, EXPERTS, TOPK, CAP, 2))(expert_ids_keys, expert_ids_turns).reshape((TOKENS, TOPK))
    gate_scale = jnp.clip(0.02 + 0.28 * jax.random.uniform(splits[11], (TOKENS, TOPK), jnp.float32) ** steps_of(splits[11], (TOKENS, TOPK), ((0, 32),), -0.2, 0.2), 0.02, 0.3)
    w_gate = gaussian(splits[12], (EXPERTS, D, FFW), D ** -0.5, 0.09375, ((0, 32), (2, 4)))
    w_up = gaussian(splits[13], (EXPERTS, D, FFW), D ** -0.5, 0.09375, ((0, 32), (2, 4)))
    w_down = gaussian(splits[14], (EXPERTS, FFW, D), FFW ** -0.5, 0.21875, ((0, 32), (1, 4)))
    return dict(residual=residual, queries=queries, new_keys=new_keys, new_values=new_values, cache_keys=cache_keys, cache_values=cache_values, new_count=new_count, cached_len=cached_len, out_proj=out_proj, norm_gain=norm_gain, expert_ids=expert_ids, gate_scale=gate_scale, w_gate=w_gate, w_up=w_up, w_down=w_down)


norm_eps = 1e-06
neg_fill = -1e+30

def attend_group(query_rows, fresh_keys, fresh_values, cache_k, cache_v, counts, lengths):
    tokens = query_rows.shape[0]
    kv_count = fresh_keys.shape[1] // HD
    per_head = query_rows.shape[1] // HD // kv_count
    convs = cache_k.shape[0]
    depth = cache_k.shape[1]
    position = jnp.arange(tokens, dtype=jnp.int32)
    run_ends = jnp.cumsum(counts).astype(jnp.int32)
    conv_of = lax.optimization_barrier(jnp.sum((position[:, None] >= run_ends[None, :]).astype(jnp.int32), axis=1)).astype(jnp.int32)
    cache_ok = (conv_of[:, None, None] == jnp.arange(convs, dtype=jnp.int32)[None, :, None]) & (jnp.arange(depth, dtype=jnp.int32)[None, None, :] < lengths[None, :, None])
    cache_ok = cache_ok.reshape(tokens, convs * depth)
    new_ok = (conv_of[:, None] == conv_of[None, :]) & (position[None, :] <= position[:, None])
    query_heads = query_rows.astype(jnp.float32).reshape(tokens, kv_count, per_head, HD)
    keys_cached = cache_k.astype(jnp.float32).reshape(convs * depth, kv_count, HD)
    values_cached = cache_v.astype(jnp.float32).reshape(convs * depth, kv_count, HD)
    keys_fresh = fresh_keys.astype(jnp.float32).reshape(tokens, kv_count, HD)
    values_fresh = fresh_values.astype(jnp.float32).reshape(tokens, kv_count, HD)
    inv_root = HD ** (-0.5)
    cache_score = jnp.einsum('tkgd,nkd->tkgn', query_heads, keys_cached) * inv_root
    fresh_score = jnp.einsum('tkgd,skd->tkgs', query_heads, keys_fresh) * inv_root
    cache_score = jnp.where(cache_ok[:, None, None, :], cache_score, neg_fill)
    fresh_score = jnp.where(new_ok[:, None, None, :], fresh_score, neg_fill)
    top_score = jnp.maximum(lax.optimization_barrier(jnp.max(cache_score, axis=-1)), lax.optimization_barrier(jnp.max(fresh_score, axis=-1)))[..., None]
    cache_exp = jnp.exp(cache_score - top_score)
    fresh_exp = jnp.exp(fresh_score - top_score)
    denom_sum = lax.optimization_barrier(jnp.sum(cache_exp, axis=-1, keepdims=True)) + lax.optimization_barrier(jnp.sum(fresh_exp, axis=-1, keepdims=True))
    cache_wts = (cache_exp / denom_sum).astype(jnp.bfloat16).astype(jnp.float32)
    fresh_wts = (fresh_exp / denom_sum).astype(jnp.bfloat16).astype(jnp.float32)
    attended = jnp.einsum('tkgn,nkd->tkgd', cache_wts, values_cached) + jnp.einsum('tkgs,skd->tkgd', fresh_wts, values_fresh)
    return attended.astype(jnp.bfloat16).reshape(tokens, kv_count * per_head * HD)

def reference(residual, queries, new_keys, new_values, cache_keys, cache_values, new_count, cached_len, out_proj, norm_gain, expert_ids, gate_scale, w_gate, w_up, w_down):
    groups = TOKENS // TOK_GRP

    def one_group(index):
        start = index * TOK_GRP
        first = index * CONV_GRP
        return attend_group(lax.dynamic_slice_in_dim(queries, start, TOK_GRP, 0), lax.dynamic_slice_in_dim(new_keys, start, TOK_GRP, 0), lax.dynamic_slice_in_dim(new_values, start, TOK_GRP, 0), lax.dynamic_slice_in_dim(cache_keys, first, CONV_GRP, 0), lax.dynamic_slice_in_dim(cache_values, first, CONV_GRP, 0), lax.dynamic_slice_in_dim(new_count, first, CONV_GRP, 0), lax.dynamic_slice_in_dim(cached_len, first, CONV_GRP, 0))
    attended = lax.map(one_group, jnp.arange(groups, dtype=jnp.int32)).reshape(TOKENS, HEADS * HD)
    projected = jnp.dot(attended, out_proj, preferred_element_type=jnp.float32)
    stream = (residual.astype(jnp.float32) + projected).astype(jnp.bfloat16)
    stream_f = stream.astype(jnp.float32)
    mean_square = lax.optimization_barrier(jnp.mean(stream_f * stream_f, axis=-1, keepdims=True))
    normed = (stream_f * lax.rsqrt(mean_square + norm_eps) * norm_gain.astype(jnp.float32)).astype(jnp.bfloat16)
    pair_ids = expert_ids.reshape(groups, TOK_GRP * TOPK)
    onehot = (pair_ids[:, :, None] == jnp.arange(EXPERTS, dtype=jnp.int32)[None, None, :]).astype(jnp.int32)
    earlier = (jnp.cumsum(onehot, axis=1).astype(jnp.int32) - onehot) * onehot
    slot_of = lax.optimization_barrier(jnp.sum(earlier, axis=2)).astype(jnp.int32)
    group_of = jnp.arange(groups, dtype=jnp.int32)[:, None]
    target = pair_ids * (groups * CAP) + group_of * CAP + slot_of
    token_of = group_of * TOK_GRP + (jnp.arange(TOK_GRP * TOPK, dtype=jnp.int32) // TOPK)[None, :]
    row_table = jnp.full((EXPERTS * groups * CAP,), TOKENS, jnp.int32).at[target.reshape(-1)].set(token_of.reshape(-1).astype(jnp.int32)).reshape(EXPERTS, groups * CAP)
    weight_table = jnp.zeros((EXPERTS * groups * CAP,), jnp.float32).at[target.reshape(-1)].set(gate_scale.reshape(-1)).reshape(EXPERTS, groups * CAP)
    normed_pad = jnp.concatenate([normed, jnp.zeros((1, D), jnp.bfloat16)], axis=0)
    quarter = FFW // N_TP

    def one_expert(mixture, inputs):
        gate_w, up_w, down_w, rows_index, row_weight = inputs
        rows_in = normed_pad[rows_index]
        gate_part = jnp.dot(rows_in, gate_w, preferred_element_type=jnp.float32)
        up_part = jnp.dot(rows_in, up_w, preferred_element_type=jnp.float32)
        activated = (jax.nn.silu(gate_part) * up_part).astype(jnp.bfloat16)
        summed = jnp.zeros((rows_in.shape[0], D), jnp.float32)
        for block in range(N_TP):
            piece = jnp.dot(activated[:, block * quarter:(block + 1) * quarter], down_w[block * quarter:(block + 1) * quarter, :], preferred_element_type=jnp.float32)
            summed = summed + lax.optimization_barrier(piece.astype(jnp.bfloat16)).astype(jnp.float32)
        expert_out = lax.optimization_barrier(summed.astype(jnp.bfloat16)).astype(jnp.float32)
        mixture = mixture.at[rows_index].add(expert_out * row_weight[:, None])
        return (mixture, None)
    mixture, _ = lax.scan(one_expert, jnp.zeros((TOKENS + 1, D), jnp.float32), (w_gate, w_up, w_down, row_table, weight_table))
    return (stream.astype(jnp.float32) + mixture[:TOKENS]).astype(jnp.bfloat16)
```

```python
import functools

import jax
import jax.numpy as jnp
from jax import lax
from jax.experimental import pallas as pl
from jax.experimental.pallas import tpu as pltpu
from jax.sharding import PartitionSpec as P

D = 4096
HD = 128
TOK = 128
CAP = 32
META = 16

norm_eps = 1e-06
neg_fill = -1e30
f32 = jnp.float32
bf16 = jnp.bfloat16
VMEM_LIMIT = 56 * 1024 * 1024


def dot(a, b, contract=((1,), (0,)), precision=None):
    return lax.dot_general(
        a, b, (contract, ((), ())), preferred_element_type=f32, precision=precision
    )


def params(*semantics):
    return pltpu.CompilerParams(
        vmem_limit_bytes=VMEM_LIMIT, dimension_semantics=semantics or None
    )


def attend_kernel(
    count_ref, len_ref, q_ref, nk_ref, nv_ref, ck_ref, cv_ref, proj_hbm, down_hbm,
    out_ref, down_out, attended, proj, sem, down_sem,
):
    parts = out_ref.shape[0]
    width = out_ref.shape[2]
    heads = q_ref.shape[1] // HD
    convs, depth = ck_ref.shape[0], ck_ref.shape[1]
    fetch = pltpu.make_async_copy(proj_hbm, proj, sem)
    fetch.start()
    regroup = [
        pltpu.make_async_copy(
            down_hbm.at[:, :, pl.ds(j * width, width)], down_out.at[j], down_sem.at[j]
        )
        for j in range(parts)
    ]
    for copy in regroup:
        copy.start()
    ends = []
    total = jnp.int32(0)
    for c in range(convs):
        total = total + count_ref[c]
        ends.append(total)
    to_exp2 = HD ** (-0.5) * 1.4426950408889634
    block = 32
    rows = heads * block
    row_tok = lax.broadcasted_iota(jnp.int32, (rows, 1), 0) % block
    col_tok = lax.broadcasted_iota(jnp.int32, (1, TOK), 1)

    def conv_of(position):
        return sum((position >= end).astype(jnp.int32) for end in ends)

    col_conv = conv_of(col_tok)
    key_pos = lax.broadcasted_iota(jnp.int32, (rows, depth), 1)
    for b in range(TOK // block):
        start = b * block
        q = jnp.concatenate(
            [q_ref[start : start + block, h * HD : (h + 1) * HD] for h in range(heads)], axis=0
        )
        tok = row_tok + start
        row_conv = conv_of(tok)
        s = dot(q, nk_ref[...], ((1,), (1,)))
        s = jnp.where((row_conv == col_conv) & (col_tok <= tok), s, neg_fill)
        top = jnp.max(s, axis=1, keepdims=True)
        p = jnp.exp2((s - top) * to_exp2)
        denom = jnp.sum(p, axis=1, keepdims=True)
        acc = dot(p.astype(bf16), nv_ref[...])
        first = conv_of(jnp.int32(start))
        last = conv_of(jnp.int32(start + block - 1))

        def step(c, carry, q=q, row_conv=row_conv):
            top, denom, acc = carry
            s = dot(q, ck_ref[c], ((1,), (1,)))
            limit = jnp.where(row_conv == c, len_ref[c], 0)
            s = jnp.where(key_pos < limit, s, neg_fill)
            new_top = jnp.maximum(top, jnp.max(s, axis=1, keepdims=True))
            p = jnp.exp2((s - new_top) * to_exp2)
            alpha = jnp.exp2((top - new_top) * to_exp2)
            denom = denom * alpha + jnp.sum(p, axis=1, keepdims=True)
            acc = acc * alpha + dot(p.astype(bf16), cv_ref[c])
            return new_top, denom, acc

        top, denom, acc = lax.fori_loop(first, last + 1, step, (top, denom, acc))
        out = (acc / denom).astype(bf16)
        for h in range(heads):
            attended[start : start + block, h * HD : (h + 1) * HD] = out[
                h * block : (h + 1) * block
            ]
    fetch.wait()
    for j in range(parts):
        out_ref[j] = dot(attended[...], proj[:, j * width : (j + 1) * width]).astype(bf16)
    for copy in regroup:
        copy.wait()


def attend(queries, new_keys, new_values, cache_keys, cache_values, new_count, cached_len, out_proj, w_down, parts):
    width = D // parts
    vmem = pl.BlockSpec(memory_space=pltpu.VMEM)
    smem = pl.BlockSpec(memory_space=pltpu.SMEM)
    hbm = pl.BlockSpec(memory_space=pl.ANY)
    return pl.pallas_call(
        attend_kernel,
        out_shape=(
            jax.ShapeDtypeStruct((parts, TOK, width), bf16),
            jax.ShapeDtypeStruct((parts,) + w_down.shape[:2] + (width,), bf16),
        ),
        in_specs=[smem, smem, vmem, vmem, vmem, vmem, vmem, hbm, hbm],
        out_specs=(vmem, hbm),
        scratch_shapes=[
            pltpu.VMEM((TOK, queries.shape[1]), bf16),
            pltpu.VMEM(out_proj.shape, bf16),
            pltpu.SemaphoreType.DMA,
            pltpu.SemaphoreType.DMA((parts,)),
        ],
        compiler_params=params(),
        name="attend",
    )(new_count, cached_len, queries, new_keys, new_values, cache_keys, cache_values, out_proj, w_down)


def thirds(v):
    high = v.astype(bf16).astype(f32)
    mid = (v - high).astype(bf16).astype(f32)
    return high, mid, v - high - mid


def prepare_kernel(at_ref, terms_ref, residual_ref, gain_ref, ids_ref, gate_ref, payload_ref, stream_ref):
    del at_ref
    total = residual_ref[...].astype(f32)
    terms = sum(terms_ref[j].astype(f32) for j in range(terms_ref.shape[0]))
    stream = (total + terms).astype(bf16)
    stream_ref[...] = stream
    s = stream.astype(f32)
    payload_ref[:TOK] = (s * gain_ref[...].astype(f32)).astype(bf16)
    square = jnp.sum(s * s, axis=1, keepdims=True)
    diagonal = lax.broadcasted_iota(jnp.int32, (TOK, TOK), 0) == lax.broadcasted_iota(
        jnp.int32, (TOK, TOK), 1
    )
    square = jnp.sum(jnp.where(diagonal, square, 0.0), axis=0, keepdims=True)
    topk = ids_ref.shape[0]

    def in_line(v):
        return jnp.concatenate([v[k : k + 1] for k in range(topk)], axis=1)

    gate = thirds(in_line(gate_ref[...]))
    blank = jnp.zeros((1, (topk - 3) * TOK), f32)
    squares = jnp.concatenate(list(thirds(square)) + [blank], axis=1)
    lines = [in_line(ids_ref[...].astype(f32)), *gate, squares]
    lines.append(jnp.zeros((META - len(lines), topk * TOK), f32))
    payload_ref[TOK:] = jnp.concatenate(lines, axis=0).astype(bf16)


def prepare(at, terms, residual, gain, ids_t, gate_t):
    width = terms.shape[2]
    return pl.pallas_call(
        prepare_kernel,
        out_shape=(
            jax.ShapeDtypeStruct((TOK + META, width), bf16),
            jax.ShapeDtypeStruct((TOK, width), bf16),
        ),
        grid_spec=pltpu.PrefetchScalarGridSpec(
            num_scalar_prefetch=1,
            grid=(1,),
            in_specs=[
                pl.BlockSpec(terms.shape, lambda i, at: (0, 0, 0)),
                pl.BlockSpec((TOK, width), lambda i, at: (0, at[0])),
                pl.BlockSpec((1, width), lambda i, at: (0, at[0])),
                pl.BlockSpec(ids_t.shape, lambda i, at: (0, 0)),
                pl.BlockSpec(gate_t.shape, lambda i, at: (0, 0)),
            ],
            out_specs=[
                pl.BlockSpec((TOK + META, width), lambda i, at: (0, 0)),
                pl.BlockSpec((TOK, width), lambda i, at: (0, 0)),
            ],
        ),
        compiler_params=params("arbitrary"),
        name="prepare",
    )(at, terms, residual, gain, ids_t, gate_t)


def experts_kernel(first_ref, x_ref, gate_w_ref, up_w_ref, act_ref, rows, groups, parts):
    width = x_ref.shape[2]
    topk = width // TOK
    local = gate_w_ref.shape[0]
    hidden = gate_w_ref.shape[2]
    earlier = (
        lax.broadcasted_iota(jnp.int32, (TOK, TOK), 0)
        < lax.broadcasted_iota(jnp.int32, (TOK, TOK), 1)
    ).astype(bf16)
    slots = lax.broadcasted_iota(jnp.int32, (CAP, TOK), 0).astype(f32)
    scales = [[], []]
    gates = [[], []]
    for g in range(groups):
        meta = x_ref[g * parts, TOK:].astype(f32)
        square = jnp.zeros((1, TOK), f32)
        for q in range(parts):
            line = (meta if q == 0 else x_ref[g * parts + q, TOK:].astype(f32))[4:5]
            square = square + (line[:, :TOK] + line[:, TOK : 2 * TOK] + line[:, 2 * TOK : 3 * TOK])
        scale = lax.rsqrt(square / D + norm_eps)
        ids = meta[0:1]
        gate = meta[1:2] + meta[2:3] + meta[3:4]
        members, weights = [], []
        for e in range(local):
            hit = ids == (first_ref[0] + e).astype(f32)
            ones = jnp.where(hit, 1.0, 0.0)
            weight = jnp.where(hit, gate, 0.0)
            members.append(sum(ones[:, k * TOK : (k + 1) * TOK] for k in range(topk)))
            weights.append(sum(weight[:, k * TOK : (k + 1) * TOK] for k in range(topk)))
        named = jnp.concatenate(members + [jnp.zeros((8 - local, TOK), f32)], axis=0)
        slot = dot(named.astype(bf16), earlier)
        picks = []
        for e in range(local):
            pick = (slots == slot[e : e + 1]) & (members[e] > 0.5)
            picks.append(jnp.where(pick, 1.0, 0.0))
            scales[e].append(jnp.sum(jnp.where(pick, scale, 0.0), axis=1, keepdims=True))
            gates[e].append(jnp.sum(jnp.where(pick, weights[e], 0.0), axis=1, keepdims=True))
        picks = jnp.concatenate(picks, axis=0).astype(bf16)
        for q in range(parts):
            picked = dot(picks, x_ref[g * parts + q, :TOK]).astype(bf16)
            for e in range(local):
                rows[e, g * CAP : (g + 1) * CAP, q * width : (q + 1) * width] = picked[
                    e * CAP : (e + 1) * CAP
                ]
    done = []
    for e in range(local):
        scale = jnp.concatenate(scales[e], axis=0)
        gate_part = dot(rows[e], gate_w_ref[e]) * scale
        up_part = dot(rows[e], up_w_ref[e]) * scale
        silu = gate_part / (1.0 + jnp.exp(-gate_part))
        done.append((silu * up_part * jnp.concatenate(gates[e], axis=0)).astype(bf16))
    act_ref[...] = jnp.concatenate(done, axis=1)


def run_experts(first, gathered, w_gate, w_up, parts):
    groups = 4
    total = gathered.shape[0] // parts
    local, _, hidden = w_gate.shape
    whole = pl.BlockSpec(w_gate.shape, lambda i: (0, 0, 0), pipeline_mode=pl.Buffered(1))
    return pl.pallas_call(
        functools.partial(experts_kernel, groups=groups, parts=parts),
        out_shape=jax.ShapeDtypeStruct((total * CAP, local * hidden), bf16),
        grid=(total // groups,),
        in_specs=[
            pl.BlockSpec(memory_space=pltpu.SMEM),
            pl.BlockSpec((groups * parts,) + gathered.shape[1:], lambda i: (i, 0, 0)),
            whole,
            whole,
        ],
        out_specs=pl.BlockSpec((groups * CAP, local * hidden), lambda i: (i, 0)),
        scratch_shapes=[pltpu.VMEM((local, groups * CAP, D), bf16)],
        compiler_params=params("arbitrary"),
        name="experts",
    )(first, gathered, w_gate, w_up)


def down_kernel(act_ref, w_ref, out_ref):
    parts, local, hidden, width = w_ref.shape
    groups = out_ref.shape[0]
    for e in range(local):
        total = sum(
            dot(act_ref[q, :, e * hidden : (e + 1) * hidden], w_ref[q, e]) for q in range(parts)
        )
        out_ref[:, e * CAP : (e + 1) * CAP] = total.astype(bf16).reshape(groups, CAP, width)


def run_down(act, w):
    parts, local, hidden, width = w.shape
    groups = 8
    total = act.shape[1] // CAP
    return pl.pallas_call(
        down_kernel,
        out_shape=jax.ShapeDtypeStruct((total, local * CAP, width), bf16),
        grid=(total // groups,),
        in_specs=[
            pl.BlockSpec((parts, groups * CAP, act.shape[2]), lambda i: (0, i, 0)),
            pl.BlockSpec(w.shape, lambda i: (0, 0, 0, 0), pipeline_mode=pl.Buffered(1)),
        ],
        out_specs=pl.BlockSpec((groups, local * CAP, width), lambda i: (i, 0, 0)),
        compiler_params=params("arbitrary"),
        name="down",
    )(act, w)


def combine_kernel(ids_ref, rows_ref, stream_ref, out_ref):
    slots = rows_ref.shape[0]
    experts = slots // CAP
    ids = ids_ref[...]
    names = lax.broadcasted_iota(jnp.int32, (TOK, experts), 1)
    member = sum((ids[:, k : k + 1] == names).astype(f32) for k in range(ids.shape[1]))
    earlier = (
        lax.broadcasted_iota(jnp.int32, (TOK, TOK), 1)
        < lax.broadcasted_iota(jnp.int32, (TOK, TOK), 0)
    ).astype(bf16)
    place = (dot(earlier, member.astype(bf16)) + 1.0) * member
    spread = (
        lax.broadcasted_iota(jnp.int32, (experts, slots), 1) // CAP
        == lax.broadcasted_iota(jnp.int32, (experts, slots), 0)
    ).astype(bf16)
    place = dot(place.astype(bf16), spread)
    own = (lax.broadcasted_iota(jnp.int32, (TOK, slots), 1) % CAP + 1).astype(f32)
    picks = (place == own).astype(bf16)
    out_ref[...] = (stream_ref[...].astype(f32) + dot(picks, rows_ref[...])).astype(bf16)


def combine(ids, rows, stream):
    vmem = pl.BlockSpec(memory_space=pltpu.VMEM)
    return pl.pallas_call(
        combine_kernel,
        out_shape=jax.ShapeDtypeStruct(stream.shape, bf16),
        in_specs=[vmem] * 3,
        out_specs=vmem,
        compiler_params=params(),
        name="combine",
    )(ids, rows, stream)


def on_device(
    residual,
    queries,
    new_keys,
    new_values,
    cache_keys,
    cache_values,
    new_count,
    cached_len,
    out_proj,
    norm_gain,
    expert_ids,
    gate_scale,
    w_gate,
    w_up,
    w_down,
):
    parts = lax.axis_size("tp")
    at = lax.axis_index("tp").astype(jnp.int32).reshape(1)
    first = (lax.axis_index("ep") * w_gate.shape[0]).astype(jnp.int32).reshape(1)
    terms, down_parts = attend(
        queries, new_keys, new_values, cache_keys, cache_values, new_count, cached_len,
        out_proj, w_down, parts,
    )
    terms = lax.all_to_all(terms, "tp", split_axis=0, concat_axis=0, tiled=True)
    down_w = lax.all_to_all(down_parts, "tp", split_axis=0, concat_axis=0, tiled=True)
    payload, stream = prepare(
        at, terms, residual, norm_gain.reshape(1, D), expert_ids.T, gate_scale.T
    )
    gathered = lax.all_gather(payload, ("ep", "tp"))
    act = run_experts(first, gathered, w_gate, w_up, parts)
    act = lax.all_gather(act, "tp")
    rows = run_down(act, down_w)
    rows = lax.all_to_all(rows, "ep", split_axis=0, concat_axis=0, tiled=True)
    return combine(expert_ids, rows.reshape(-1, rows.shape[2]), stream)


def solution(mesh):
    in_specs = (
        P("ep", None),
        P("ep", "tp"),
        P("ep", "tp"),
        P("ep", "tp"),
        P("ep", None, "tp"),
        P("ep", None, "tp"),
        P("ep"),
        P("ep"),
        P("tp", None),
        P(),
        P("ep", None),
        P("ep", None),
        P("ep", None, "tp"),
        P("ep", None, "tp"),
        P("ep", "tp", None),
    )
    out_specs = P("ep", "tp")
    return jax.shard_map(
        on_device, mesh=mesh, in_specs=in_specs, out_specs=out_specs, check_vma=False
    )
```

```python
import functools

import jax
import jax.numpy as jnp
from jax import lax
from jax.experimental import pallas as pl
from jax.experimental.pallas import tpu as pltpu
from jax.sharding import PartitionSpec as P

D = 4096
HD = 128
TOK = 128
CAP = 32
META = 16

norm_eps = 1e-06
neg_fill = -1e30
f32 = jnp.float32
bf16 = jnp.bfloat16
VMEM_LIMIT = 56 * 1024 * 1024


def dot(a, b, contract=((1,), (0,)), precision=None):
    return lax.dot_general(
        a, b, (contract, ((), ())), preferred_element_type=f32, precision=precision
    )


def params(*semantics):
    return pltpu.CompilerParams(
        vmem_limit_bytes=VMEM_LIMIT, dimension_semantics=semantics or None
    )


def cost(flops, size):
    return pl.CostEstimate(flops=int(flops), bytes_accessed=int(size), transcendentals=0)


def attend_kernel(
    at_ref, count_ref, len_ref, q_ref, nk_ref, nv_ref, ck_ref, cv_ref, proj_hbm, *rest, parts
):
    out_refs = rest[:parts]
    attended, proj, sem = rest[parts:]
    width = out_refs[0].shape[1]
    heads = q_ref.shape[1] // HD
    convs, depth = ck_ref.shape[0], ck_ref.shape[1]
    fetch = pltpu.make_async_copy(proj_hbm, proj, sem)
    fetch.start()
    ends = []
    total = jnp.int32(0)
    for c in range(convs):
        total = total + count_ref[c]
        ends.append(total)
    to_exp2 = HD ** (-0.5) * 1.4426950408889634
    block = 32
    rows = heads * block
    row_tok = lax.broadcasted_iota(jnp.int32, (rows, 1), 0) % block
    col_tok = lax.broadcasted_iota(jnp.int32, (1, TOK), 1)

    def conv_of(position):
        return sum((position >= end).astype(jnp.int32) for end in ends)

    col_conv = conv_of(col_tok)
    key_pos = lax.broadcasted_iota(jnp.int32, (rows, depth), 1)
    for b in range(TOK // block):
        start = b * block
        q = jnp.concatenate(
            [q_ref[start : start + block, h * HD : (h + 1) * HD] for h in range(heads)], axis=0
        )
        tok = row_tok + start
        row_conv = conv_of(tok)
        s = dot(q, nk_ref[...], ((1,), (1,)))
        s = jnp.where((row_conv == col_conv) & (col_tok <= tok), s, neg_fill)
        top = jnp.max(s, axis=1, keepdims=True)
        p = jnp.exp2((s - top) * to_exp2)
        denom = jnp.sum(p, axis=1, keepdims=True)
        acc = dot(p.astype(bf16), nv_ref[...])
        first = conv_of(jnp.int32(start))
        last = conv_of(jnp.int32(start + block - 1))

        def step(c, carry, q=q, row_conv=row_conv):
            top, denom, acc = carry
            s = dot(q, ck_ref[c], ((1,), (1,)))
            limit = jnp.where(row_conv == c, len_ref[c], 0)
            s = jnp.where(key_pos < limit, s, neg_fill)
            new_top = jnp.maximum(top, jnp.max(s, axis=1, keepdims=True))
            p = jnp.exp2((s - new_top) * to_exp2)
            alpha = jnp.exp2((top - new_top) * to_exp2)
            denom = denom * alpha + jnp.sum(p, axis=1, keepdims=True)
            acc = acc * alpha + dot(p.astype(bf16), cv_ref[c])
            return new_top, denom, acc

        top, denom, acc = lax.fori_loop(first, last + 1, step, (top, denom, acc))
        out = (acc / denom).astype(bf16)
        for h in range(heads):
            attended[start : start + block, h * HD : (h + 1) * HD] = out[
                h * block : (h + 1) * block
            ]
    fetch.wait()
    for j in range(parts):
        to = pl.multiple_of(lax.rem(at_ref[0] + j, parts) * width, width)
        out_refs[j][...] = dot(attended[...], proj[:, pl.ds(to, width)]).astype(bf16)


def attend(at, queries, new_keys, new_values, cache_keys, cache_values, new_count, cached_len, out_proj, parts):
    width = D // parts
    vmem = pl.BlockSpec(memory_space=pltpu.VMEM)
    smem = pl.BlockSpec(memory_space=pltpu.SMEM)
    hbm = pl.BlockSpec(memory_space=pl.ANY)
    return pl.pallas_call(
        functools.partial(attend_kernel, parts=parts),
        out_shape=[jax.ShapeDtypeStruct((TOK, width), bf16)] * parts,
        in_specs=[smem, smem, smem, vmem, vmem, vmem, vmem, vmem, hbm],
        out_specs=[vmem] * parts,
        scratch_shapes=[
            pltpu.VMEM((TOK, queries.shape[1]), bf16),
            pltpu.VMEM(out_proj.shape, bf16),
            pltpu.SemaphoreType.DMA,
        ],
        compiler_params=params(),
        name="attend",
    )(at, new_count, cached_len, queries, new_keys, new_values, cache_keys, cache_values, out_proj)


def thirds(v):
    high = v.astype(bf16).astype(f32)
    mid = (v - high).astype(bf16).astype(f32)
    return high, mid, v - high - mid


def prepare_kernel(at_ref, *refs, parts):
    terms_refs = refs[:parts]
    residual_ref, gain_ref, ids_ref, gate_ref, payload_ref, stream_ref, at_out = refs[parts:]
    at_out[0] = at_ref[0]
    total = residual_ref[...].astype(f32)
    terms = sum(ref[...].astype(f32) for ref in terms_refs)
    stream = (total + terms).astype(bf16)
    stream_ref[...] = stream
    s = stream.astype(f32)
    payload_ref[:TOK] = (s * gain_ref[...].astype(f32)).astype(bf16)
    square = jnp.sum(s * s, axis=1, keepdims=True)
    diagonal = lax.broadcasted_iota(jnp.int32, (TOK, TOK), 0) == lax.broadcasted_iota(
        jnp.int32, (TOK, TOK), 1
    )
    square = jnp.sum(jnp.where(diagonal, square, 0.0), axis=0, keepdims=True)
    topk = ids_ref.shape[0]

    def in_line(v):
        return jnp.concatenate([v[k : k + 1] for k in range(topk)], axis=1)

    gate = thirds(in_line(gate_ref[...]))
    blank = jnp.zeros((1, (topk - 3) * TOK), f32)
    squares = jnp.concatenate(list(thirds(square)) + [blank], axis=1)
    lines = [in_line(ids_ref[...].astype(f32)), *gate, squares]
    lines.append(jnp.zeros((META - len(lines), topk * TOK), f32))
    payload_ref[TOK:] = jnp.concatenate(lines, axis=0).astype(bf16)


def prepare(at, terms, residual, gain, ids_t, gate_t):
    parts = len(terms)
    width = terms[0].shape[1]
    return pl.pallas_call(
        functools.partial(prepare_kernel, parts=parts),
        out_shape=(
            jax.ShapeDtypeStruct((TOK + META, width), bf16),
            jax.ShapeDtypeStruct((TOK, width), bf16),
            jax.ShapeDtypeStruct((1,), jnp.int32),
        ),
        grid_spec=pltpu.PrefetchScalarGridSpec(
            num_scalar_prefetch=1,
            grid=(1,),
            in_specs=[pl.BlockSpec((TOK, width), lambda i, at: (0, 0))] * parts
            + [
                pl.BlockSpec((TOK, width), lambda i, at: (0, at[0])),
                pl.BlockSpec((1, width), lambda i, at: (0, at[0])),
                pl.BlockSpec(ids_t.shape, lambda i, at: (0, 0)),
                pl.BlockSpec(gate_t.shape, lambda i, at: (0, 0)),
            ],
            out_specs=[
                pl.BlockSpec((TOK + META, width), lambda i, at: (0, 0)),
                pl.BlockSpec((TOK, width), lambda i, at: (0, 0)),
                pl.BlockSpec(memory_space=pltpu.SMEM),
            ],
        ),
        compiler_params=params("arbitrary"),
        name="prepare",
    )(at, *terms, residual, gain, ids_t, gate_t)


def experts_kernel(first_ref, x_ref, gate_w_ref, up_w_ref, *refs, groups, parts, held):
    act_ref, rows = refs[held:]
    width = x_ref.shape[2]
    topk = width // TOK
    local = gate_w_ref.shape[0]
    pair = 2
    earlier = (
        lax.broadcasted_iota(jnp.int32, (TOK, TOK), 0)
        < lax.broadcasted_iota(jnp.int32, (TOK, TOK), 1)
    ).astype(bf16)
    slots = lax.broadcasted_iota(jnp.int32, (CAP, TOK), 0).astype(f32)
    scales = [[] for _ in range(local)]
    gates = [[] for _ in range(local)]
    picks = [[] for _ in range(local)]
    for g in range(groups):
        meta = x_ref[g * parts, TOK:].astype(f32)
        square = jnp.zeros((1, TOK), f32)
        for q in range(parts):
            line = (meta if q == 0 else x_ref[g * parts + q, TOK:].astype(f32))[4:5]
            square = square + (line[:, :TOK] + line[:, TOK : 2 * TOK] + line[:, 2 * TOK : 3 * TOK])
        scale = lax.rsqrt(square / D + norm_eps)
        ids = meta[0:1]
        gate = meta[1:2] + meta[2:3] + meta[3:4]
        members, weights = [], []
        for e in range(local):
            hit = ids == (first_ref[0] + e).astype(f32)
            ones = jnp.where(hit, 1.0, 0.0)
            weight = jnp.where(hit, gate, 0.0)
            members.append(sum(ones[:, k * TOK : (k + 1) * TOK] for k in range(topk)))
            weights.append(sum(weight[:, k * TOK : (k + 1) * TOK] for k in range(topk)))
        named = jnp.concatenate(members + [jnp.zeros((8 - local, TOK), f32)], axis=0)
        slot = dot(named.astype(bf16), earlier)
        for e in range(local):
            pick = (slots == slot[e : e + 1]) & (members[e] > 0.5)
            picks[e].append(jnp.where(pick, 1.0, 0.0))
            scales[e].append(jnp.sum(jnp.where(pick, scale, 0.0), axis=1, keepdims=True))
            gates[e].append(jnp.sum(jnp.where(pick, weights[e], 0.0), axis=1, keepdims=True))
    size = pair * CAP
    blank = jnp.zeros((CAP, TOK), f32)
    for g in range(0, groups, pair):
        lines = []
        for e in range(local):
            for i in range(pair):
                line = [picks[e][g + i] if j == i else blank for j in range(pair)]
                lines.append(jnp.concatenate(line, axis=1))
        pick = jnp.concatenate(lines, axis=0).astype(bf16)
        for q in range(parts):
            x = jnp.concatenate([x_ref[(g + i) * parts + q, :TOK] for i in range(pair)], axis=0)
            picked = dot(pick, x).astype(bf16)
            for e in range(local):
                rows[e, g * CAP : g * CAP + size, q * width : (q + 1) * width] = picked[
                    e * size : (e + 1) * size
                ]
    done = []
    for e in range(local):
        scale = jnp.concatenate(scales[e], axis=0)
        gate_part = dot(rows[e], gate_w_ref[e]) * scale
        up_part = dot(rows[e], up_w_ref[e]) * scale
        silu = gate_part / (1.0 + jnp.exp(-gate_part))
        done.append((silu * up_part * jnp.concatenate(gates[e], axis=0)).astype(bf16))
    act_ref[...] = jnp.concatenate(done, axis=1)


def run_experts(first, gathered, w_gate, w_up, held, parts, chunk, chunks):
    groups = 4
    steps = gathered.shape[0] // parts // groups // chunks
    local, _, hidden = w_gate.shape
    whole = pl.BlockSpec(w_gate.shape, lambda i: (0, 0, 0), pipeline_mode=pl.Buffered(1))
    return pl.pallas_call(
        functools.partial(experts_kernel, groups=groups, parts=parts, held=len(held)),
        out_shape=jax.ShapeDtypeStruct((steps * groups * CAP, local * hidden), bf16),
        grid=(steps,),
        in_specs=[
            pl.BlockSpec(memory_space=pltpu.SMEM),
            pl.BlockSpec((groups * parts,) + gathered.shape[1:], lambda i: (chunk * steps + i, 0, 0)),
            whole,
            whole,
        ]
        + [pl.BlockSpec(memory_space=pl.ANY)] * len(held),
        out_specs=pl.BlockSpec((groups * CAP, local * hidden), lambda i: (i, 0)),
        scratch_shapes=[pltpu.VMEM((local, groups * CAP, D), bf16)],
        compiler_params=params("arbitrary"),
        cost_estimate=cost(7e9, gathered.size) if chunk == 0 else cost(1, 1),
        name="experts",
    )(first, gathered, w_gate, w_up, *held)


def down_kernel(*refs, parts):
    act_refs, w_refs, out_ref = refs[:parts], refs[parts : 2 * parts], refs[-1]
    local, hidden, width = w_refs[0].shape
    groups = out_ref.shape[0]
    for e in range(local):
        total = sum(
            dot(act_refs[q][:, e * hidden : (e + 1) * hidden], w_refs[q][e]) for q in range(parts)
        )
        out_ref[:, e * CAP : (e + 1) * CAP] = total.astype(bf16).reshape(groups, CAP, width)


def run_down(acts, ws, chunk, chunks, filled):
    local, hidden, width = ws[0].shape
    groups = 8
    held = [] if filled is None else [filled]
    total = acts[0].shape[0] // CAP * chunks
    steps = total // groups // chunks
    return pl.pallas_call(
        functools.partial(down_kernel, parts=len(acts)),
        out_shape=jax.ShapeDtypeStruct((total, local * CAP, width), bf16),
        grid=(steps,),
        in_specs=[pl.BlockSpec((groups * CAP, local * hidden), lambda i: (i, 0))] * len(acts)
        + [pl.BlockSpec(ws[0].shape, lambda i: (0, 0, 0), pipeline_mode=pl.Buffered(1))] * len(ws)
        + [pl.BlockSpec(memory_space=pl.ANY)] * len(held),
        out_specs=pl.BlockSpec(
            (groups, local * CAP, width), lambda i: (chunk * steps + i, 0, 0)
        ),
        input_output_aliases={2 * len(acts): 0} if held else {},
        compiler_params=params("arbitrary"),
        cost_estimate=cost(1, 1),
        name="down",
    )(*acts, *ws, *held)


def place_kernel(ids_ref, picks_ref):
    slots = picks_ref.shape[1]
    experts = slots // CAP
    ids = ids_ref[...]
    names = lax.broadcasted_iota(jnp.int32, (TOK, experts), 1)
    member = sum((ids[:, k : k + 1] == names).astype(f32) for k in range(ids.shape[1]))
    earlier = (
        lax.broadcasted_iota(jnp.int32, (TOK, TOK), 1)
        < lax.broadcasted_iota(jnp.int32, (TOK, TOK), 0)
    ).astype(bf16)
    place = (dot(earlier, member.astype(bf16)) + 1.0) * member
    spread = (
        lax.broadcasted_iota(jnp.int32, (experts, slots), 1) // CAP
        == lax.broadcasted_iota(jnp.int32, (experts, slots), 0)
    ).astype(bf16)
    place = dot(place.astype(bf16), spread)
    own = (lax.broadcasted_iota(jnp.int32, (TOK, slots), 1) % CAP + 1).astype(f32)
    picks_ref[...] = (place == own).astype(bf16)


def places(ids, slots):
    vmem = pl.BlockSpec(memory_space=pltpu.VMEM)
    return pl.pallas_call(
        place_kernel,
        out_shape=jax.ShapeDtypeStruct((TOK, slots), bf16),
        in_specs=[vmem],
        out_specs=vmem,
        compiler_params=params(),
        cost_estimate=cost(1e8, 1e6),
        name="places",
    )(ids)


def combine_kernel(picks_ref, rows_ref, stream_ref, out_ref, total):
    @pl.when(pl.program_id(0) == 0)
    def _():
        total[...] = stream_ref[...].astype(f32)

    total[...] += dot(picks_ref[...], rows_ref[...])

    @pl.when(pl.program_id(0) == pl.num_programs(0) - 1)
    def _():
        out_ref[...] = total[...].astype(bf16)


def combine(picks, rows, stream):
    steps = 2
    size = rows.shape[0] // steps
    whole = pl.BlockSpec(stream.shape, lambda i: (0, 0))
    return pl.pallas_call(
        combine_kernel,
        out_shape=jax.ShapeDtypeStruct(stream.shape, bf16),
        grid=(steps,),
        in_specs=[
            pl.BlockSpec((TOK, size), lambda i: (0, i)),
            pl.BlockSpec((size, rows.shape[1]), lambda i: (i, 0)),
            whole,
        ],
        out_specs=whole,
        scratch_shapes=[pltpu.VMEM(stream.shape, f32)],
        compiler_params=params("arbitrary"),
        name="combine",
    )(picks, rows, stream)


def on_device(
    residual,
    queries,
    new_keys,
    new_values,
    cache_keys,
    cache_values,
    new_count,
    cached_len,
    out_proj,
    norm_gain,
    expert_ids,
    gate_scale,
    w_gate,
    w_up,
    w_down,
):
    parts = lax.axis_size("tp")
    at = lax.axis_index("tp").astype(jnp.int32).reshape(1)
    first = (lax.axis_index("ep") * w_gate.shape[0]).astype(jnp.int32).reshape(1)
    local = w_gate.shape[0]
    width = D // parts

    def shift(v, by):
        return lax.ppermute(v, "tp", [(i, (i + by) % parts) for i in range(parts)])

    def spread(vs):
        return [vs[0]] + [shift(vs[j], j) for j in range(1, parts)]

    terms = spread(
        attend(
            at, queries, new_keys, new_values, cache_keys, cache_values, new_count, cached_len,
            out_proj, parts,
        )
    )
    payload, stream, at = prepare(
        at, terms, residual, norm_gain.reshape(1, D), expert_ids.T, gate_scale.T
    )
    gathered = lax.all_gather(payload, ("ep", "tp"))
    down_w = spread(
        [
            lax.dynamic_slice_in_dim(w_down, lax.rem(at[0] + j, parts) * width, width, 2)
            for j in range(parts)
        ]
    )
    picks = places(expert_ids, lax.axis_size("ep") * local * CAP)
    chunks = 2
    held = [*down_w, picks]
    acts = []
    for chunk in range(chunks):
        acts.append(run_experts(first, gathered, w_gate, w_up, held, parts, chunk, chunks))
        held = acts[-1:]
    rows = None
    for chunk, act in enumerate(acts):
        rows = run_down(spread([act] * parts), down_w, chunk, chunks, rows)
    rows = lax.all_to_all(rows, "ep", split_axis=0, concat_axis=0, tiled=True)
    return combine(picks, rows.reshape(-1, width), stream)


def solution(mesh):
    in_specs = (
        P("ep", None),
        P("ep", "tp"),
        P("ep", "tp"),
        P("ep", "tp"),
        P("ep", None, "tp"),
        P("ep", None, "tp"),
        P("ep"),
        P("ep"),
        P("tp", None),
        P(),
        P("ep", None),
        P("ep", None),
        P("ep", None, "tp"),
        P("ep", None, "tp"),
        P("ep", "tp", None),
    )
    out_specs = P("ep", "tp")
    return jax.shard_map(
        on_device, mesh=mesh, in_specs=in_specs, out_specs=out_specs, check_vma=False
    )
```

```python
import functools

import jax
import jax.numpy as jnp
from jax import lax
from jax.experimental import pallas as pl
from jax.experimental.pallas import tpu as pltpu
from jax.sharding import PartitionSpec as P

D = 4096
HD = 128
TOK = 128
CAP = 32
META = 8
SIDE = 4
CORES = 2

norm_eps = 1e-06
neg_fill = -1e30
f32 = jnp.float32
bf16 = jnp.bfloat16


def dot(a, b, contract=((1,), (0,)), precision=None):
    return lax.dot_general(
        a, b, (contract, ((), ())), preferred_element_type=f32, precision=precision
    )


def params(*semantics, limit=56):
    return pltpu.CompilerParams(
        vmem_limit_bytes=limit * 1024 * 1024, dimension_semantics=semantics or None
    )


def cost(flops, size):
    return pl.CostEstimate(flops=int(flops), bytes_accessed=int(size), transcendentals=0)


def attend_kernel(
    at_ref, count_ref, len_ref, q_ref, nk_ref, nv_ref, ck_ref, cv_ref, proj_hbm, *rest, parts
):
    out_refs = rest[:parts]
    attended, proj, sem = rest[parts:]
    width = out_refs[0].shape[1]
    heads = q_ref.shape[1] // HD
    convs, depth = ck_ref.shape[0], ck_ref.shape[1]
    fetch = pltpu.make_async_copy(proj_hbm, proj, sem)
    fetch.start()
    ends = []
    total = jnp.int32(0)
    for c in range(convs):
        total = total + count_ref[c]
        ends.append(total)
    to_exp2 = HD ** (-0.5) * 1.4426950408889634
    block = 32
    rows = heads * block
    row_tok = lax.broadcasted_iota(jnp.int32, (rows, 1), 0) % block
    col_tok = lax.broadcasted_iota(jnp.int32, (1, TOK), 1)

    def conv_of(position):
        return sum((position >= end).astype(jnp.int32) for end in ends)

    col_conv = conv_of(col_tok)
    key_pos = lax.broadcasted_iota(jnp.int32, (rows, depth), 1)
    for b in range(TOK // block):
        start = b * block
        q = jnp.concatenate(
            [q_ref[start : start + block, h * HD : (h + 1) * HD] for h in range(heads)], axis=0
        )
        tok = row_tok + start
        row_conv = conv_of(tok)
        s = dot(q, nk_ref[...], ((1,), (1,)))
        s = jnp.where((row_conv == col_conv) & (col_tok <= tok), s, neg_fill)
        top = jnp.max(s, axis=1, keepdims=True)
        p = jnp.exp2((s - top) * to_exp2)
        denom = jnp.sum(p, axis=1, keepdims=True)
        acc = dot(p.astype(bf16), nv_ref[...])
        first = conv_of(jnp.int32(start))
        last = conv_of(jnp.int32(start + block - 1))

        def step(c, carry, q=q, row_conv=row_conv):
            top, denom, acc = carry
            s = dot(q, ck_ref[c], ((1,), (1,)))
            limit = jnp.where(row_conv == c, len_ref[c], 0)
            s = jnp.where(key_pos < limit, s, neg_fill)
            new_top = jnp.maximum(top, jnp.max(s, axis=1, keepdims=True))
            p = jnp.exp2((s - new_top) * to_exp2)
            alpha = jnp.exp2((top - new_top) * to_exp2)
            denom = denom * alpha + jnp.sum(p, axis=1, keepdims=True)
            acc = acc * alpha + dot(p.astype(bf16), cv_ref[c])
            return new_top, denom, acc

        top, denom, acc = lax.fori_loop(first, last + 1, step, (top, denom, acc))
        out = (acc / denom).astype(bf16)
        for h in range(heads):
            attended[start : start + block, h * HD : (h + 1) * HD] = out[
                h * block : (h + 1) * block
            ]
    fetch.wait()
    for j in range(parts):
        to = pl.multiple_of(lax.rem(at_ref[0] + j, parts) * width, width)
        out_refs[j][...] = dot(attended[...], proj[:, pl.ds(to, width)]).astype(bf16)


def attend(at, queries, new_keys, new_values, cache_keys, cache_values, new_count, cached_len, out_proj, parts):
    width = D // parts
    vmem = pl.BlockSpec(memory_space=pltpu.VMEM)
    smem = pl.BlockSpec(memory_space=pltpu.SMEM)
    hbm = pl.BlockSpec(memory_space=pl.ANY)
    return pl.pallas_call(
        functools.partial(attend_kernel, parts=parts),
        out_shape=[jax.ShapeDtypeStruct((TOK, width), bf16)] * parts,
        in_specs=[smem, smem, smem, vmem, vmem, vmem, vmem, vmem, hbm],
        out_specs=[vmem] * parts,
        scratch_shapes=[
            pltpu.VMEM((TOK, queries.shape[1]), bf16),
            pltpu.VMEM(out_proj.shape, bf16),
            pltpu.SemaphoreType.DMA,
        ],
        compiler_params=params(),
        name="attend",
    )(at, new_count, cached_len, queries, new_keys, new_values, cache_keys, cache_values, out_proj)


def thirds(v):
    high = v.astype(bf16).astype(f32)
    mid = (v - high).astype(bf16).astype(f32)
    return high, mid, v - high - mid


def prepare_kernel(at_ref, *refs, parts):
    terms_refs = refs[:parts]
    residual_ref, gain_ref, ids_ref, gate_ref, payload_ref, stream_ref, at_out = refs[parts:]
    at_out[0] = at_ref[0]
    total = residual_ref[...].astype(f32)
    terms = sum(ref[...].astype(f32) for ref in terms_refs)
    stream = (total + terms).astype(bf16)
    stream_ref[...] = stream
    s = stream.astype(f32)
    payload_ref[:TOK] = (s * gain_ref[...].astype(f32)).astype(bf16)
    square = jnp.sum(s * s, axis=1, keepdims=True)
    diagonal = lax.broadcasted_iota(jnp.int32, (TOK, TOK), 0) == lax.broadcasted_iota(
        jnp.int32, (TOK, TOK), 1
    )
    square = jnp.sum(jnp.where(diagonal, square, 0.0), axis=0, keepdims=True)
    topk = ids_ref.shape[0]

    def in_line(v):
        return jnp.concatenate([v[k : k + 1] for k in range(topk)], axis=1)

    gate = thirds(in_line(gate_ref[...]))
    blank = jnp.zeros((1, (topk - 3) * TOK), f32)
    squares = jnp.concatenate(list(thirds(square)) + [blank], axis=1)
    lines = [in_line(ids_ref[...].astype(f32)), *gate, squares]
    lines.append(jnp.zeros((META - len(lines), topk * TOK), f32))
    payload_ref[TOK:] = jnp.concatenate(lines, axis=0).astype(bf16)


def prepare(at, terms, residual, gain, ids_t, gate_t):
    parts = len(terms)
    width = terms[0].shape[1]
    return pl.pallas_call(
        functools.partial(prepare_kernel, parts=parts),
        out_shape=(
            jax.ShapeDtypeStruct((TOK + META, width), bf16),
            jax.ShapeDtypeStruct((TOK, width), bf16),
            jax.ShapeDtypeStruct((1,), jnp.int32),
        ),
        grid_spec=pltpu.PrefetchScalarGridSpec(
            num_scalar_prefetch=1,
            grid=(1,),
            in_specs=[pl.BlockSpec((TOK, width), lambda i, at: (0, 0))] * parts
            + [
                pl.BlockSpec((TOK, width), lambda i, at: (0, at[0])),
                pl.BlockSpec((1, width), lambda i, at: (0, at[0])),
                pl.BlockSpec(ids_t.shape, lambda i, at: (0, 0)),
                pl.BlockSpec(gate_t.shape, lambda i, at: (0, 0)),
            ],
            out_specs=[
                pl.BlockSpec((TOK + META, width), lambda i, at: (0, 0)),
                pl.BlockSpec((TOK, width), lambda i, at: (0, 0)),
                pl.BlockSpec(memory_space=pltpu.SMEM),
            ],
        ),
        compiler_params=params("arbitrary"),
        name="prepare",
    )(at, *terms, residual, gain, ids_t, gate_t)


def experts_kernel(at_ref, x_ref, own_ref, peer_ref, *refs, parts, held):
    act_ref, picks_ref, rows = refs[held:]
    groups = x_ref.shape[0]
    width = x_ref.shape[5]
    topk = width // TOK
    local = own_ref.shape[0]
    hidden = own_ref.shape[2] // 2
    names = [at_ref[0] + e for e in range(local)] + [at_ref[1] + e for e in range(local)]
    count = len(names)
    pair = 2
    earlier = (
        lax.broadcasted_iota(jnp.int32, (TOK, TOK), 0)
        < lax.broadcasted_iota(jnp.int32, (TOK, TOK), 1)
    ).astype(bf16)
    slots = lax.broadcasted_iota(jnp.int32, (CAP, TOK), 0).astype(f32)
    scales = [[] for _ in names]
    gates = [[] for _ in names]
    picks = [[] for _ in names]
    for g in range(groups):
        meta = x_ref[g, 0, 0, 0, TOK:].astype(f32)
        square = jnp.zeros((1, TOK), f32)
        for q in range(parts):
            line = (meta if q == 0 else x_ref[g, 0, 0, q, TOK:].astype(f32))[4:5]
            square = square + (line[:, :TOK] + line[:, TOK : 2 * TOK] + line[:, 2 * TOK : 3 * TOK])
        scale = lax.rsqrt(square / D + norm_eps)
        ids = meta[0:1]
        gate = meta[1:2] + meta[2:3] + meta[3:4]
        members, weights = [], []
        for name in names:
            hit = ids == name.astype(f32)
            ones = jnp.where(hit, 1.0, 0.0)
            weight = jnp.where(hit, gate, 0.0)
            members.append(sum(ones[:, k * TOK : (k + 1) * TOK] for k in range(topk)))
            weights.append(sum(weight[:, k * TOK : (k + 1) * TOK] for k in range(topk)))
        named = jnp.concatenate(members + [jnp.zeros((8 - count, TOK), f32)], axis=0)
        slot = dot(named.astype(bf16), earlier)
        for e in range(count):
            pick = (slots == slot[e : e + 1]) & (members[e] > 0.5)
            picks[e].append(jnp.where(pick, 1.0, 0.0))
            scales[e].append(jnp.sum(jnp.where(pick, scale, 0.0), axis=1, keepdims=True))
            gates[e].append(jnp.sum(jnp.where(pick, weights[e], 0.0), axis=1, keepdims=True))
        picks_ref[g] = jnp.concatenate([picks[e][g] for e in range(count)], axis=0).astype(bf16)
    size = pair * CAP
    blank = jnp.zeros((CAP, TOK), f32)
    for g in range(0, groups, pair):
        lines = []
        for e in range(count):
            for i in range(pair):
                line = [picks[e][g + i] if j == i else blank for j in range(pair)]
                lines.append(jnp.concatenate(line, axis=1))
        pick = jnp.concatenate(lines, axis=0).astype(bf16)
        for q in range(parts):
            x = jnp.concatenate([x_ref[g + i, 0, 0, q, :TOK] for i in range(pair)], axis=0)
            picked = dot(pick, x).astype(bf16)
            for e in range(count):
                rows[e, g * CAP : g * CAP + size, q * width : (q + 1) * width] = picked[
                    e * size : (e + 1) * size
                ]
    done = []
    for e in range(count):
        w_ref = own_ref if e < local else peer_ref
        both = dot(rows[e], w_ref[e % local]) * jnp.concatenate(scales[e], axis=0)
        gate_part, up_part = both[:, :hidden], both[:, hidden:]
        silu = gate_part / (1.0 + jnp.exp(-gate_part))
        done.append((silu * up_part * jnp.concatenate(gates[e], axis=0)).astype(bf16))
    act_ref[...] = jnp.concatenate(done, axis=1)


def run_experts(at, gathered, own_w, peer_w, held, chunk, chunks):
    groups = gathered.shape[0]
    parts = gathered.shape[3]
    steps = SIDE // chunks
    local, _, hidden = own_w.shape
    hidden = hidden // 2
    count = CORES * local
    whole = pl.BlockSpec(memory_space=pltpu.VMEM)
    return pl.pallas_call(
        functools.partial(experts_kernel, parts=parts, held=len(held)),
        out_shape=(
            jax.ShapeDtypeStruct((steps * groups * CAP, count * hidden), bf16),
            jax.ShapeDtypeStruct((steps * groups, count * CAP, TOK), bf16),
        ),
        grid_spec=pltpu.PrefetchScalarGridSpec(
            num_scalar_prefetch=1,
            grid=(steps,),
            in_specs=[
                pl.BlockSpec(
                    (groups, 1, 1) + gathered.shape[3:],
                    lambda i, at: (
                        0, lax.rem(at[3] + 1 + chunk * steps + i, SIDE), at[4], 0, 0, 0
                    ),
                ),
                whole,
                whole,
            ]
            + [pl.BlockSpec(memory_space=pl.ANY)] * len(held),
            out_specs=[
                pl.BlockSpec((groups * CAP, count * hidden), lambda i, at: (i, 0)),
                pl.BlockSpec((groups, count * CAP, TOK), lambda i, at: (i, 0, 0)),
            ],
            scratch_shapes=[pltpu.VMEM((count, groups * CAP, D), bf16)],
        ),
        compiler_params=params("arbitrary", limit=32),
        cost_estimate=cost(7e9, gathered.size) if chunk == 0 else cost(1, 1),
        name="experts",
    )(at, gathered, own_w, peer_w, *held)


def down_kernel(at_ref, *refs, parts, sets):
    act_refs, picks_ref = refs[:parts], refs[parts]
    rows = refs[-1]
    out_refs = refs[-1 - sets - SIDE : -1]
    w_refs = refs[parts + 1 : -1 - sets - SIDE]
    local, hidden, width = w_refs[0].shape
    count = CORES * local
    half = width // 2
    for e in range(count):
        block = w_refs[e // local * parts : (e // local + 1) * parts]
        total = sum(
            dot(act_refs[q][:, e * hidden : (e + 1) * hidden], block[q][e % local])
            for q in range(parts)
        )
        rows[e] = total.astype(bf16)
    for along_z in range(sets):
        for j in range(SIDE):
            g = along_z * SIDE + lax.rem(at_ref[2] + j, SIDE)
            at = pl.multiple_of(g * CAP, CAP)
            own = jnp.concatenate([rows[e, pl.ds(at, CAP)] for e in range(count)], axis=0)
            summed = dot(picks_ref[g], own, ((0,), (0,))).astype(bf16)
            out_refs[along_z][j] = summed[:, :half]
            out_refs[sets + j][along_z] = summed[:, half:]


def run_down(at, acts, picks, ws, sets):
    local, hidden, width = ws[0].shape
    vmem = pl.BlockSpec(memory_space=pltpu.VMEM)
    outs = [jax.ShapeDtypeStruct((SIDE, TOK, width // 2), bf16)] * sets
    outs += [jax.ShapeDtypeStruct((sets, TOK, width // 2), bf16)] * SIDE
    outs = pl.pallas_call(
        functools.partial(down_kernel, parts=len(acts), sets=sets),
        out_shape=outs,
        in_specs=[pl.BlockSpec(memory_space=pltpu.SMEM)] + [vmem] * (len(acts) + 1 + len(ws)),
        out_specs=[vmem] * len(outs),
        scratch_shapes=[pltpu.VMEM((CORES * local, acts[0].shape[0], width), bf16)],
        compiler_params=params(),
        cost_estimate=cost(1, 1),
        name="down",
    )(at, *acts, picks, *ws)
    return outs[:sets], outs[sets:]


def sum_kernel(*refs, z_count, chunks):
    z_refs = refs[:z_count]
    y_refs = refs[z_count : z_count + SIDE * chunks]
    outs = refs[z_count + SIDE * chunks :]
    for j in range(SIDE):
        outs[j][...] = sum(ref[j].astype(f32) for ref in z_refs).astype(bf16)
    sets = SIDE // chunks
    for j in range(SIDE):
        chunk, row = divmod((j - 1) % SIDE, sets)
        refs_of = y_refs[chunk * SIDE : (chunk + 1) * SIDE]
        outs[SIDE + j][...] = sum(ref[row].astype(f32) for ref in refs_of).astype(bf16)


def sum_along(z_blocks, y_blocks):
    vmem = pl.BlockSpec(memory_space=pltpu.VMEM)
    blocks = z_blocks + [block for chunk in y_blocks for block in chunk]
    outs = pl.pallas_call(
        functools.partial(sum_kernel, z_count=len(z_blocks), chunks=len(y_blocks)),
        out_shape=[jax.ShapeDtypeStruct(blocks[0].shape[1:], bf16)] * (2 * SIDE),
        in_specs=[vmem] * len(blocks),
        out_specs=[vmem] * (2 * SIDE),
        compiler_params=params(),
        name="sum_along",
    )(*blocks)
    return outs[:SIDE], outs[SIDE:]


def total_kernel(stream_ref, *refs):
    out_ref = refs[-1]
    half = out_ref.shape[1] // 2
    count = (len(refs) - 1) // 2
    for i, at in enumerate((0, half)):
        part = sum(ref[...].astype(f32) for ref in refs[i * count : (i + 1) * count])
        part = stream_ref[:, at : at + half].astype(f32) + part
        out_ref[:, at : at + half] = part.astype(bf16)


def total_of(stream, left, right):
    vmem = pl.BlockSpec(memory_space=pltpu.VMEM)
    return pl.pallas_call(
        total_kernel,
        out_shape=jax.ShapeDtypeStruct(stream.shape, bf16),
        in_specs=[vmem] * (1 + len(left) + len(right)),
        out_specs=vmem,
        compiler_params=params(),
        name="total",
    )(stream, *left, *right)


def on_device(
    residual,
    queries,
    new_keys,
    new_values,
    cache_keys,
    cache_values,
    new_count,
    cached_len,
    out_proj,
    norm_gain,
    expert_ids,
    gate_scale,
    w_gate,
    w_up,
    w_down,
):
    parts = lax.axis_size("tp")
    at = lax.axis_index("tp").astype(jnp.int32).reshape(1)
    ep = lax.axis_index("ep").astype(jnp.int32)
    local = w_gate.shape[0]
    width = D // parts
    core = ep % CORES
    peer = ep + 1 - 2 * core
    place = jnp.stack(
        [ep * local, peer * local, ep // (CORES * SIDE), ep // CORES % SIDE, core]
    )

    def shift(v, by):
        return lax.ppermute(v, "tp", [(i, (i + by) % parts) for i in range(parts)])

    def spread(vs):
        return [vs[0]] + [shift(vs[j], j) for j in range(1, parts)]

    def shift_ep(v, dy, dz, dc):
        def index(y, z, c):
            return (y % SIDE * SIDE + z % SIDE) * CORES + c % CORES

        pairs = [
            (index(y, z, c), index(y + dy, z + dz, c + dc))
            for y in range(SIDE)
            for z in range(SIDE)
            for c in range(CORES)
        ]
        return lax.ppermute(v, "ep", pairs)

    def columns_of(part):
        return lax.dynamic_slice_in_dim(w_down, lax.rem(part, parts) * width, width, 2)

    def flag(v):
        return (v[(0,) * v.ndim] > 1e30).astype(jnp.int32)

    near = {j: columns_of(at[0] + j) for j in (1, parts - 1)}
    ahead = at + sum(flag(v) for v in near.values())
    near = {j: shift(v, j) for j, v in near.items()}
    terms = spread(
        attend(
            ahead, queries, new_keys, new_values, cache_keys, cache_values, new_count, cached_len,
            out_proj, parts,
        )
    )
    at = at + sum(flag(v) for v in near.values())
    payload, stream, behind = prepare(
        at, terms, residual, norm_gain.reshape(1, D), expert_ids.T, gate_scale.T
    )
    gathered = lax.all_gather(payload, ("ep", "tp"))
    gathered = gathered.reshape((SIDE, SIDE, CORES, parts) + payload.shape)
    own_w = jnp.concatenate([w_gate, w_up], axis=2)
    peer_w = jnp.concatenate([shift_ep(w, 0, 0, 1) for w in (w_gate, w_up)], axis=2)
    behind = behind[0]
    down_w = [columns_of(behind)] + [
        near[j] if j in near else shift(columns_of(behind + j), j) for j in range(1, parts)
    ]
    down_w = down_w + [shift_ep(block, 0, 0, 1) for block in down_w]
    chunks = 2
    sets = SIDE // chunks
    held = down_w
    made = []
    for chunk in range(chunks):
        made.append(run_experts(place, gathered, own_w, peer_w, held, chunk, chunks))
        held = [made[-1][0]]
    by_z, by_y = [], []
    for act, picks in made:
        along_z, along_y = run_down(place, spread([act] * parts), picks, down_w, sets)
        by_z += along_z
        by_y.append([along_y[0]] + [shift_ep(along_y[j], j, 0, 0) for j in range(1, SIDE)])
    by_z = [by_z[-1]] + [shift_ep(block, 0, j + 1, 0) for j, block in enumerate(by_z[:-1])]
    left, right = sum_along(by_z, by_y)
    left = [left[0]] + [shift_ep(left[j], j, 0, 0) for j in range(1, SIDE)]
    right = [right[0]] + [shift_ep(right[j], 0, j, 0) for j in range(1, SIDE)]
    return total_of(stream, left, right)


def solution(mesh):
    in_specs = (
        P("ep", None),
        P("ep", "tp"),
        P("ep", "tp"),
        P("ep", "tp"),
        P("ep", None, "tp"),
        P("ep", None, "tp"),
        P("ep"),
        P("ep"),
        P("tp", None),
        P(),
        P("ep", None),
        P("ep", None),
        P("ep", None, "tp"),
        P("ep", None, "tp"),
        P("ep", "tp", None),
    )
    out_specs = P("ep", "tp")
    return jax.shard_map(
        on_device, mesh=mesh, in_specs=in_specs, out_specs=out_specs, check_vma=False
    )
```

```python
import functools

import jax
import jax.numpy as jnp
from jax import lax
from jax.experimental import pallas as pl
from jax.experimental.pallas import tpu as pltpu
from jax.sharding import PartitionSpec as P

D = 4096
HD = 128
TOK = 128
CAP = 32
META = 8
SIDE = 4
CORES = 2

norm_eps = 1e-06
neg_fill = -1e30
f32 = jnp.float32
bf16 = jnp.bfloat16


def dot(a, b, contract=((1,), (0,)), precision=None):
    return lax.dot_general(
        a, b, (contract, ((), ())), preferred_element_type=f32, precision=precision
    )


def params(*semantics, limit=56):
    return pltpu.CompilerParams(
        vmem_limit_bytes=limit * 1024 * 1024, dimension_semantics=semantics or None
    )


def cost(flops, size):
    return pl.CostEstimate(flops=int(flops), bytes_accessed=int(size), transcendentals=0)


def attend_kernel(
    at_ref, count_ref, len_ref, q_ref, nk_ref, nv_ref, ck_ref, cv_ref, proj_hbm, *rest, parts
):
    out_refs = rest[:parts]
    attended, proj, sem = rest[parts:]
    width = out_refs[0].shape[1]
    heads = q_ref.shape[1] // HD
    convs, depth = ck_ref.shape[0], ck_ref.shape[1]
    fetch = pltpu.make_async_copy(proj_hbm, proj, sem)
    fetch.start()
    ends = []
    total = jnp.int32(0)
    for c in range(convs):
        total = total + count_ref[c]
        ends.append(total)
    to_exp2 = HD ** (-0.5) * 1.4426950408889634
    block = 32
    rows = heads * block
    row_tok = lax.broadcasted_iota(jnp.int32, (rows, 1), 0) % block
    col_tok = lax.broadcasted_iota(jnp.int32, (1, TOK), 1)

    def conv_of(position):
        return sum((position >= end).astype(jnp.int32) for end in ends)

    col_conv = conv_of(col_tok)
    key_pos = lax.broadcasted_iota(jnp.int32, (rows, depth), 1)
    for b in range(TOK // block):
        start = b * block
        q = jnp.concatenate(
            [q_ref[start : start + block, h * HD : (h + 1) * HD] for h in range(heads)], axis=0
        )
        tok = row_tok + start
        row_conv = conv_of(tok)
        s = dot(q, nk_ref[...], ((1,), (1,)))
        s = jnp.where((row_conv == col_conv) & (col_tok <= tok), s, neg_fill)
        top = jnp.max(s, axis=1, keepdims=True)
        p = jnp.exp2((s - top) * to_exp2)
        denom = jnp.sum(p, axis=1, keepdims=True)
        acc = dot(p.astype(bf16), nv_ref[...])
        first = conv_of(jnp.int32(start))
        last = conv_of(jnp.int32(start + block - 1))

        def step(c, carry, q=q, row_conv=row_conv):
            top, denom, acc = carry
            s = dot(q, ck_ref[c], ((1,), (1,)))
            limit = jnp.where(row_conv == c, len_ref[c], 0)
            s = jnp.where(key_pos < limit, s, neg_fill)
            new_top = jnp.maximum(top, jnp.max(s, axis=1, keepdims=True))
            p = jnp.exp2((s - new_top) * to_exp2)
            alpha = jnp.exp2((top - new_top) * to_exp2)
            denom = denom * alpha + jnp.sum(p, axis=1, keepdims=True)
            acc = acc * alpha + dot(p.astype(bf16), cv_ref[c])
            return new_top, denom, acc

        top, denom, acc = lax.fori_loop(first, last + 1, step, (top, denom, acc))
        out = (acc / denom).astype(bf16)
        for h in range(heads):
            attended[start : start + block, h * HD : (h + 1) * HD] = out[
                h * block : (h + 1) * block
            ]
    fetch.wait()
    for j in range(parts):
        to = pl.multiple_of(lax.rem(at_ref[0] + j, parts) * width, width)
        out_refs[j][...] = dot(attended[...], proj[:, pl.ds(to, width)]).astype(bf16)


def attend(at, queries, new_keys, new_values, cache_keys, cache_values, new_count, cached_len, out_proj, parts):
    width = D // parts
    vmem = pl.BlockSpec(memory_space=pltpu.VMEM)
    smem = pl.BlockSpec(memory_space=pltpu.SMEM)
    hbm = pl.BlockSpec(memory_space=pl.ANY)
    return pl.pallas_call(
        functools.partial(attend_kernel, parts=parts),
        out_shape=[jax.ShapeDtypeStruct((TOK, width), bf16)] * parts,
        in_specs=[smem, smem, smem, vmem, vmem, vmem, vmem, vmem, hbm],
        out_specs=[vmem] * parts,
        scratch_shapes=[
            pltpu.VMEM((TOK, queries.shape[1]), bf16),
            pltpu.VMEM(out_proj.shape, bf16),
            pltpu.SemaphoreType.DMA,
        ],
        compiler_params=params(),
        name="attend",
    )(at, new_count, cached_len, queries, new_keys, new_values, cache_keys, cache_values, out_proj)


def thirds(v):
    high = v.astype(bf16).astype(f32)
    mid = (v - high).astype(bf16).astype(f32)
    return high, mid, v - high - mid


def prepare_kernel(at_ref, *refs, parts):
    terms_refs = refs[:parts]
    residual_ref, gain_ref, ids_ref, gate_ref, payload_ref, stream_ref, at_out = refs[parts:]
    at_out[0] = at_ref[0]
    total = residual_ref[...].astype(f32)
    terms = sum(ref[...].astype(f32) for ref in terms_refs)
    stream = (total + terms).astype(bf16)
    stream_ref[...] = stream
    s = stream.astype(f32)
    payload_ref[:TOK] = (s * gain_ref[...].astype(f32)).astype(bf16)
    square = jnp.sum(s * s, axis=1, keepdims=True)
    diagonal = lax.broadcasted_iota(jnp.int32, (TOK, TOK), 0) == lax.broadcasted_iota(
        jnp.int32, (TOK, TOK), 1
    )
    square = jnp.sum(jnp.where(diagonal, square, 0.0), axis=0, keepdims=True)
    topk = ids_ref.shape[0]

    def in_line(v):
        return jnp.concatenate([v[k : k + 1] for k in range(topk)], axis=1)

    gate = thirds(in_line(gate_ref[...]))
    blank = jnp.zeros((1, (topk - 3) * TOK), f32)
    squares = jnp.concatenate(list(thirds(square)) + [blank], axis=1)
    lines = [in_line(ids_ref[...].astype(f32)), *gate, squares]
    lines.append(jnp.zeros((META - len(lines), topk * TOK), f32))
    payload_ref[TOK:] = jnp.concatenate(lines, axis=0).astype(bf16)


def prepare(at, terms, residual, gain, ids_t, gate_t):
    parts = len(terms)
    width = terms[0].shape[1]
    return pl.pallas_call(
        functools.partial(prepare_kernel, parts=parts),
        out_shape=(
            jax.ShapeDtypeStruct((TOK + META, width), bf16),
            jax.ShapeDtypeStruct((TOK, width), bf16),
            jax.ShapeDtypeStruct((1,), jnp.int32),
        ),
        grid_spec=pltpu.PrefetchScalarGridSpec(
            num_scalar_prefetch=1,
            grid=(1,),
            in_specs=[pl.BlockSpec((TOK, width), lambda i, at: (0, 0))] * parts
            + [
                pl.BlockSpec((TOK, width), lambda i, at: (0, at[0])),
                pl.BlockSpec((1, width), lambda i, at: (0, at[0])),
                pl.BlockSpec(ids_t.shape, lambda i, at: (0, 0)),
                pl.BlockSpec(gate_t.shape, lambda i, at: (0, 0)),
            ],
            out_specs=[
                pl.BlockSpec((TOK + META, width), lambda i, at: (0, 0)),
                pl.BlockSpec((TOK, width), lambda i, at: (0, 0)),
                pl.BlockSpec(memory_space=pltpu.SMEM),
            ],
        ),
        compiler_params=params("arbitrary"),
        name="prepare",
    )(at, *terms, residual, gain, ids_t, gate_t)


def experts_kernel(at_ref, x_ref, own_hbm, peer_hbm, *refs, parts, held):
    act_ref, picks_ref, rows, both_w, sems = refs[held:]
    groups = x_ref.shape[0]
    width = x_ref.shape[5]
    topk = width // TOK
    local = own_hbm.shape[0]
    hidden = own_hbm.shape[2] // 2
    names = [at_ref[0] + e for e in range(local)] + [at_ref[1] + e for e in range(local)]
    count = len(names)
    pair = 2
    fetch = [
        pltpu.make_async_copy(
            (own_hbm if e < local else peer_hbm).at[e % local], both_w.at[e], sems.at[e]
        )
        for e in range(count)
    ]

    @pl.when(pl.program_id(0) == 0)
    def _():
        for copy in fetch:
            copy.start()

    earlier = (
        lax.broadcasted_iota(jnp.int32, (TOK, TOK), 0)
        < lax.broadcasted_iota(jnp.int32, (TOK, TOK), 1)
    ).astype(bf16)
    slots = lax.broadcasted_iota(jnp.int32, (CAP, TOK), 0).astype(f32)
    scales = [[] for _ in names]
    gates = [[] for _ in names]
    picks = [[] for _ in names]
    for g in range(groups):
        meta = x_ref[g, 0, 0, 0, TOK:].astype(f32)
        square = jnp.zeros((1, TOK), f32)
        for q in range(parts):
            line = (meta if q == 0 else x_ref[g, 0, 0, q, TOK:].astype(f32))[4:5]
            square = square + (line[:, :TOK] + line[:, TOK : 2 * TOK] + line[:, 2 * TOK : 3 * TOK])
        scale = lax.rsqrt(square / D + norm_eps)
        ids = meta[0:1]
        gate = meta[1:2] + meta[2:3] + meta[3:4]
        members, weights = [], []
        for name in names:
            hit = ids == name.astype(f32)
            ones = jnp.where(hit, 1.0, 0.0)
            weight = jnp.where(hit, gate, 0.0)
            members.append(sum(ones[:, k * TOK : (k + 1) * TOK] for k in range(topk)))
            weights.append(sum(weight[:, k * TOK : (k + 1) * TOK] for k in range(topk)))
        named = jnp.concatenate(members + [jnp.zeros((8 - count, TOK), f32)], axis=0)
        slot = dot(named.astype(bf16), earlier)
        for e in range(count):
            pick = (slots == slot[e : e + 1]) & (members[e] > 0.5)
            picks[e].append(jnp.where(pick, 1.0, 0.0))
            scales[e].append(jnp.sum(jnp.where(pick, scale, 0.0), axis=1, keepdims=True))
            gates[e].append(jnp.sum(jnp.where(pick, weights[e], 0.0), axis=1, keepdims=True))
        named = jnp.concatenate([picks[e][g] for e in range(count)], axis=0)
        picks_ref[g] = named.T.astype(bf16)
    size = pair * CAP
    blank = jnp.zeros((CAP, TOK), f32)
    for g in range(0, groups, pair):
        lines = []
        for e in range(count):
            for i in range(pair):
                line = [picks[e][g + i] if j == i else blank for j in range(pair)]
                lines.append(jnp.concatenate(line, axis=1))
        pick = jnp.concatenate(lines, axis=0).astype(bf16)
        for q in range(parts):
            x = jnp.concatenate([x_ref[g + i, 0, 0, q, :TOK] for i in range(pair)], axis=0)
            picked = dot(pick, x).astype(bf16)
            for e in range(count):
                rows[e, g * CAP : g * CAP + size, q * width : (q + 1) * width] = picked[
                    e * size : (e + 1) * size
                ]
    done = []
    for e in range(count):
        pl.when(pl.program_id(0) == 0)(fetch[e].wait)
        both = dot(rows[e], both_w[e]) * jnp.concatenate(scales[e], axis=0)
        gate_part, up_part = both[:, :hidden], both[:, hidden:]
        silu = gate_part / (1.0 + jnp.exp(-gate_part))
        done.append((silu * up_part * jnp.concatenate(gates[e], axis=0)).astype(bf16))
    act_ref[...] = jnp.concatenate(done, axis=1)


def run_experts(at, gathered, own_w, peer_w, held, chunk, chunks):
    groups = gathered.shape[0]
    parts = gathered.shape[3]
    steps = SIDE // chunks
    local, _, hidden = own_w.shape
    hidden = hidden // 2
    count = CORES * local
    hbm = pl.BlockSpec(memory_space=pl.ANY)
    return pl.pallas_call(
        functools.partial(experts_kernel, parts=parts, held=len(held)),
        out_shape=(
            jax.ShapeDtypeStruct((steps * groups * CAP, count * hidden), bf16),
            jax.ShapeDtypeStruct((steps * groups, TOK, count * CAP), bf16),
        ),
        grid_spec=pltpu.PrefetchScalarGridSpec(
            num_scalar_prefetch=1,
            grid=(steps,),
            in_specs=[
                pl.BlockSpec(
                    (groups, 1, 1) + gathered.shape[3:],
                    lambda i, at: (
                        0, lax.rem(at[3] + 1 + chunk * steps + i, SIDE), at[4], 0, 0, 0
                    ),
                ),
            ]
            + [hbm] * (2 + len(held)),
            out_specs=[
                pl.BlockSpec((groups * CAP, count * hidden), lambda i, at: (i, 0)),
                pl.BlockSpec((groups, TOK, count * CAP), lambda i, at: (i, 0, 0)),
            ],
            scratch_shapes=[
                pltpu.VMEM((count, groups * CAP, D), bf16),
                pltpu.VMEM((count,) + own_w.shape[1:], bf16),
                pltpu.SemaphoreType.DMA((count,)),
            ],
        ),
        compiler_params=params("arbitrary", limit=44),
        cost_estimate=cost(7e9, gathered.size) if chunk == 0 else cost(1, 1),
        name="experts",
    )(at, gathered, own_w, peer_w, *held)


def down_kernel(at_ref, *refs, parts, sets):
    act_refs, picks_ref = refs[:parts], refs[parts]
    rows = refs[-1]
    out_refs = refs[-1 - sets - SIDE : -1]
    w_refs = refs[parts + 1 : -1 - sets - SIDE]
    local, hidden, width = w_refs[0].shape
    count = CORES * local
    half = width // 2
    for e in range(count):
        block = w_refs[e // local * parts : (e // local + 1) * parts]
        total = sum(
            dot(act_refs[q][:, e * hidden : (e + 1) * hidden], block[q][e % local])
            for q in range(parts)
        )
        rows[e] = total.astype(bf16)
    for along_z in range(sets):
        for j in range(SIDE):
            g = along_z * SIDE + lax.rem(at_ref[2] + j, SIDE)
            at = pl.multiple_of(g * CAP, CAP)
            own = jnp.concatenate([rows[e, pl.ds(at, CAP)] for e in range(count)], axis=0)
            summed = dot(picks_ref[g], own).astype(bf16)
            out_refs[along_z][j] = summed[:, :half]
            out_refs[sets + j][along_z] = summed[:, half:]


def run_down(at, acts, picks, ws, sets):
    local, hidden, width = ws[0].shape
    vmem = pl.BlockSpec(memory_space=pltpu.VMEM)
    outs = [jax.ShapeDtypeStruct((SIDE, TOK, width // 2), bf16)] * sets
    outs += [jax.ShapeDtypeStruct((sets, TOK, width // 2), bf16)] * SIDE
    outs = pl.pallas_call(
        functools.partial(down_kernel, parts=len(acts), sets=sets),
        out_shape=outs,
        in_specs=[pl.BlockSpec(memory_space=pltpu.SMEM)] + [vmem] * (len(acts) + 1 + len(ws)),
        out_specs=[vmem] * len(outs),
        scratch_shapes=[pltpu.VMEM((CORES * local, acts[0].shape[0], width), bf16)],
        compiler_params=params(),
        cost_estimate=cost(1, 1),
        name="down",
    )(at, *acts, picks, *ws)
    return outs[:sets], outs[sets:]


def sum_kernel(*refs, z_count, chunks):
    z_refs = refs[:z_count]
    y_refs = refs[z_count : z_count + SIDE * chunks]
    outs = refs[z_count + SIDE * chunks :]
    for j in range(SIDE):
        outs[j][...] = sum(ref[j].astype(f32) for ref in z_refs).astype(bf16)
    sets = SIDE // chunks
    for j in range(SIDE):
        chunk, row = divmod((j - 1) % SIDE, sets)
        refs_of = y_refs[chunk * SIDE : (chunk + 1) * SIDE]
        outs[SIDE + j][...] = sum(ref[row].astype(f32) for ref in refs_of).astype(bf16)


def sum_along(z_blocks, y_blocks):
    vmem = pl.BlockSpec(memory_space=pltpu.VMEM)
    blocks = z_blocks + [block for chunk in y_blocks for block in chunk]
    outs = pl.pallas_call(
        functools.partial(sum_kernel, z_count=len(z_blocks), chunks=len(y_blocks)),
        out_shape=[jax.ShapeDtypeStruct(blocks[0].shape[1:], bf16)] * (2 * SIDE),
        in_specs=[vmem] * len(blocks),
        out_specs=[vmem] * (2 * SIDE),
        compiler_params=params(),
        name="sum_along",
    )(*blocks)
    return outs[:SIDE], outs[SIDE:]


def total_kernel(stream_ref, *refs):
    out_ref = refs[-1]
    half = out_ref.shape[1] // 2
    count = (len(refs) - 1) // 2
    for i, at in enumerate((0, half)):
        part = sum(ref[...].astype(f32) for ref in refs[i * count : (i + 1) * count])
        part = stream_ref[:, at : at + half].astype(f32) + part
        out_ref[:, at : at + half] = part.astype(bf16)


def total_of(stream, left, right):
    vmem = pl.BlockSpec(memory_space=pltpu.VMEM)
    return pl.pallas_call(
        total_kernel,
        out_shape=jax.ShapeDtypeStruct(stream.shape, bf16),
        in_specs=[vmem] * (1 + len(left) + len(right)),
        out_specs=vmem,
        compiler_params=params(),
        name="total",
    )(stream, *left, *right)


def on_device(
    residual,
    queries,
    new_keys,
    new_values,
    cache_keys,
    cache_values,
    new_count,
    cached_len,
    out_proj,
    norm_gain,
    expert_ids,
    gate_scale,
    w_gate,
    w_up,
    w_down,
):
    parts = lax.axis_size("tp")
    at = lax.axis_index("tp").astype(jnp.int32).reshape(1)
    ep = lax.axis_index("ep").astype(jnp.int32)
    local = w_gate.shape[0]
    width = D // parts
    core = ep % CORES
    peer = ep + 1 - 2 * core
    place = jnp.stack(
        [ep * local, peer * local, ep // (CORES * SIDE), ep // CORES % SIDE, core]
    )

    def shift(v, by):
        return lax.ppermute(v, "tp", [(i, (i + by) % parts) for i in range(parts)])

    def spread(vs):
        return [vs[0]] + [shift(vs[j], j) for j in range(1, parts)]

    def shift_ep(v, dy, dz, dc):
        def index(y, z, c):
            return (y % SIDE * SIDE + z % SIDE) * CORES + c % CORES

        pairs = [
            (index(y, z, c), index(y + dy, z + dz, c + dc))
            for y in range(SIDE)
            for z in range(SIDE)
            for c in range(CORES)
        ]
        return lax.ppermute(v, "ep", pairs)

    def columns_of(part):
        return lax.dynamic_slice_in_dim(w_down, lax.rem(part, parts) * width, width, 2)

    def flag(v):
        return (v[(0,) * v.ndim] > 1e30).astype(jnp.int32)

    near = {j: columns_of(at[0] + j) for j in (1, parts - 1)}
    near = {j: shift(v, j) for j, v in near.items()}
    terms = spread(
        attend(
            at, queries, new_keys, new_values, cache_keys, cache_values, new_count, cached_len,
            out_proj, parts,
        )
    )
    at = at + sum(flag(v) for v in near.values())
    payload, stream, behind = prepare(
        at, terms, residual, norm_gain.reshape(1, D), expert_ids.T, gate_scale.T
    )
    gathered = lax.all_gather(payload, ("ep", "tp"))
    gathered = gathered.reshape((SIDE, SIDE, CORES, parts) + payload.shape)
    own_w = jnp.concatenate([w_gate, w_up], axis=2)
    peer_w = jnp.concatenate([shift_ep(w, 0, 0, 1) for w in (w_gate, w_up)], axis=2)
    behind = behind[0]
    down_w = [columns_of(behind)] + [
        near[j] if j in near else shift(columns_of(behind + j), j) for j in range(1, parts)
    ]
    down_w = down_w + [shift_ep(block, 0, 0, 1) for block in down_w]
    chunks = 2
    sets = SIDE // chunks
    held = down_w
    made = []
    for chunk in range(chunks):
        made.append(run_experts(place, gathered, own_w, peer_w, held, chunk, chunks))
        held = [made[-1][0]]
    by_z, by_y = [], []
    for act, picks in made:
        along_z, along_y = run_down(place, spread([act] * parts), picks, down_w, sets)
        by_z += along_z
        by_y.append([along_y[0]] + [shift_ep(along_y[j], j, 0, 0) for j in range(1, SIDE)])
    by_z = [by_z[-1]] + [shift_ep(block, 0, j + 1, 0) for j, block in enumerate(by_z[:-1])]
    left, right = sum_along(by_z, by_y)
    left = [left[0]] + [shift_ep(left[j], j, 0, 0) for j in range(1, SIDE)]
    right = [right[0]] + [shift_ep(right[j], 0, j, 0) for j in range(1, SIDE)]
    return total_of(stream, left, right)


def solution(mesh):
    in_specs = (
        P("ep", None),
        P("ep", "tp"),
        P("ep", "tp"),
        P("ep", "tp"),
        P("ep", None, "tp"),
        P("ep", None, "tp"),
        P("ep"),
        P("ep"),
        P("tp", None),
        P(),
        P("ep", None),
        P("ep", None),
        P("ep", None, "tp"),
        P("ep", None, "tp"),
        P("ep", "tp", None),
    )
    out_specs = P("ep", "tp")
    return jax.shard_map(
        on_device, mesh=mesh, in_specs=in_specs, out_specs=out_specs, check_vma=False
    )
```
